32 devices in a mesh: pairs: 16 (over z, y, x), aux: 2 (over core).
Axes of the slice: x: 2, y: 2, z: 4, core: 2. Of those that a mesh axis runs over, the one named last changes fastest.
Arguments:
- densities: bfloat16 [16, 12288], P(None, 'pairs'), may hold values from -6 to 6
- tensor: bfloat16 [12288, 20480], P('pairs', 'aux'), may hold values from -0.078125 to 0.078125
- metric: bfloat16 [20480, 20480], P('aux', 'pairs'), may hold values from -0.0390625 to 0.0390625
- row_count: int32 [16], P('pairs'), may hold values from 1 to 768, 7680 in all
Outputs:
- coulomb: bfloat16 [16, 12288], P('aux', 'pairs')
The draws below stay inside these ranges and needn't reach their ends.
Inputs may be any that keep to these rules, and one draw needn't show every extreme that they name: The first row_count[b] rows of pair block b are live; some block has all 768 rows live.
All inputs are finite; a program needn't handle non-finite values.
Results may differ from the reference program's by a relative error of at most 0.0057.
Values may be sent and summed in bfloat16 or wider, within the bound.
No kernel may reach another device: no remote copies, remote signals or barrier semaphores. Data moves between devices by JAX's collectives and lax.ppermute only.
A program may use at most 128 MiB of HBM per device.

```python
import math
import jax
import jax.numpy as jnp
import numpy as np
from jax import lax

NAUX = 20480
K = 16
ROWS_DEV = 768
ROWS = 12288
N_PAIRS = 16


def with_spikes(entries, key, source, target, parts, factor):
    owner, partner = [(jnp.arange(entries.shape[position]) // (entries.shape[position] // parts)).reshape([-1 if axis == position else 1 for axis in range(entries.ndim)]) for position in (source, target)]
    chosen = jax.random.permutation(key, parts)[partner]
    strong = (owner == chosen) | (owner == (partner + parts // 2) % parts)
    return jnp.where(strong, factor * entries, entries)


def levels(rng, shape, cuts, smallest, high):
    loudness = 1.0
    for axis_at, blocks in cuts:
        heights = jax.random.uniform(jax.random.fold_in(jax.random.fold_in(rng, 6), axis_at), (blocks,), jnp.float32, smallest / len(cuts), high / len(cuts))
        loudness = loudness * jnp.repeat(jnp.exp(heights), shape[axis_at] // blocks).reshape((-1,) + (1,) * (len(shape) - 1 - axis_at))
    return loudness


def length_profile(count, total, limit, slope):
    loads = [(1 << 20) // math.isqrt(rank ** slope) + 1 for rank in range(2, count + 1)]
    spare, holding = total - limit - (count - 1), [1] * (count - 1)
    while spare > 0:
        free = [i for i in range(count - 1) if holding[i] < limit]
        mass, budget = sum([loads[i] for i in free]), spare
        for i in free:
            addition = min(limit - holding[i], max(1, budget * loads[i] // mass), spare)
            holding[i] = holding[i] + addition
            spare = spare - addition
    return np.array([limit] + holding)


def uneven_parts(rng, number_of, total, most, slope):
    if number_of == 2:
        one = jax.random.randint(rng, (), max(1, total - most), min(most, total - 1) + 1)
        return jnp.stack([one, total - one])
    tallies = jnp.asarray(length_profile(number_of, total, most, slope), jnp.int32)
    pairs = (number_of - 1) // 2
    donor, taker = tallies[1:1 + 2 * pairs:2], tallies[2:2 + 2 * pairs:2]
    margin = jnp.minimum(donor - 1, most - taker)
    passed = jax.random.randint(jax.random.fold_in(rng, 1), (pairs,), 0, 1 << 20) % (margin + 1)
    tallies = tallies.at[1:1 + 2 * pairs:2].set(donor - passed).at[2:2 + 2 * pairs:2].set(taker + passed)
    return tallies[jax.random.permutation(jax.random.fold_in(rng, 2), number_of)]


def scatter_about(own_key, dims, scale, limit, shards=(), kind=jnp.bfloat16):
    level = levels(own_key, dims, shards, -0.22, 0.18) if shards else 1.0
    entries = jax.random.normal(own_key, dims, jnp.float32) * scale * level
    return jnp.minimum(jnp.maximum(entries, -limit), limit).astype(kind)


def bell_draw_with(own_key, dims, scale, limit, shards, heavy, held_as=jnp.bfloat16):
    array = scale * jax.random.normal(own_key, dims, jnp.float32)
    if shards:
        array = array * levels(own_key, dims, shards, -0.22, 0.18)
    return jnp.clip(with_spikes(array, jax.random.fold_in(own_key, 3), *heavy), -limit, limit).astype(held_as)


def setup_inputs(seed: int = 0) -> dict:
    splits = jax.random.split(jax.random.key(seed), 5)
    return {
        "densities": scatter_about(splits[0], (K, ROWS), 1.0, 6.0, ((1, 16),)),
        "tensor": bell_draw_with(splits[1], (ROWS, NAUX), ROWS ** -0.5, 0.078125, ((0, 16), (1, 2)), (0, 1, 16, 2.0)),
        "metric": scatter_about(splits[2], (NAUX, NAUX), NAUX ** -0.5, 0.0390625, ((0, 2), (1, 16))),
        "row_count": uneven_parts(splits[3], N_PAIRS, ROWS_DEV * N_PAIRS * 5 // 8, ROWS_DEV, 2).astype(jnp.int32),
    }


def reference(densities, tensor, metric, row_count):
    blocks = tensor.reshape(N_PAIRS, ROWS_DEV, NAUX)
    dense_blocks = densities.reshape(K, N_PAIRS, ROWS_DEV).transpose(1, 0, 2)
    positions = jnp.arange(ROWS_DEV, dtype=jnp.int32)
    live = positions[None, :] < row_count[:, None].astype(jnp.int32)

    def add_block(total, items):
        block, dense, alive = items
        masked = jnp.where(alive[None, :], dense, jnp.zeros_like(dense))
        term = jnp.dot(masked.astype(jnp.float32), block.astype(jnp.float32), precision=lax.Precision.HIGHEST)
        return total + term, None

    fitted, _ = lax.scan(add_block, jnp.zeros((K, NAUX), jnp.float32), (blocks, dense_blocks, live))
    fitted = fitted.astype(jnp.bfloat16)
    metric_rows = metric.reshape(N_PAIRS, NAUX // N_PAIRS, NAUX)
    fitted_rows = fitted.reshape(K, N_PAIRS, NAUX // N_PAIRS).transpose(1, 0, 2)

    def add_metric(total, items):
        rows_here, fit_here = items
        term = jnp.dot(fit_here.astype(jnp.float32), rows_here.astype(jnp.float32), precision=lax.Precision.HIGHEST)
        return total + term, None

    solved, _ = lax.scan(add_metric, jnp.zeros((K, NAUX), jnp.float32), (metric_rows, fitted_rows))
    solved = solved.astype(jnp.bfloat16).astype(jnp.float32)

    def back_block(items):
        block, alive = items
        term = jnp.dot(solved, block.astype(jnp.float32).T, precision=lax.Precision.HIGHEST)
        return jnp.where(alive[None, :], term, jnp.zeros_like(term))

    result = lax.map(back_block, (blocks, live))
    return result.transpose(1, 0, 2).reshape(K, N_PAIRS * ROWS_DEV).astype(jnp.bfloat16)
```

```python
import functools

import jax
import jax.numpy as jnp
from jax import lax
from jax.experimental import pallas as pl
from jax.experimental.pallas import tpu as pltpu
from jax.sharding import PartitionSpec as P

F32, BF16 = jnp.float32, jnp.bfloat16
MIB = 1 << 20


def digits_of(count):
    sizes = []
    while count > 1:
        size = 4 if count % 4 == 0 else 2
        sizes.append(size)
        count //= size
    return sizes


def largest_step(extent, limit, unit):
    return max(s for s in range(unit, limit + 1, unit) if extent % s == 0)


def swap(x, axis, count, mask):
    return lax.ppermute(x, axis, [(i, i ^ mask) for i in range(count)])


def params(used_bytes):
    return pltpu.CompilerParams(vmem_limit_bytes=used_bytes + 4 * MIB)


def fit_kernel(picks, step, digit_ref, count_ref, dens_ref, tensor_ref, *rest):
    outs, (held, sems) = rest[: len(picks)], rest[len(picks) :]
    width = outs[0].shape[1]
    copies = []
    for at, pick in enumerate(picks):
        first = (digit_ref[0] ^ pick) * width
        for j in range(width // step):
            slot = at * (width // step) + j
            copy = pltpu.make_async_copy(
                tensor_ref.at[:, pl.ds(pl.multiple_of(first + j * step, 128), step)],
                held.at[slot],
                sems.at[slot],
            )
            copy.start()
            copies.append(copy)
    dens = dens_ref[...]
    live = lax.broadcasted_iota(jnp.int32, dens.shape, 1) < count_ref[0]
    masked = jnp.where(live, dens.astype(F32), 0.0).astype(BF16)
    for at in range(len(picks)):
        for j in range(width // step):
            slot = at * (width // step) + j
            copies[slot].wait()
            term = jnp.dot(masked, held[slot], preferred_element_type=F32)
            outs[at][:, j * step : (j + 1) * step] = term.astype(outs[at].dtype)


def fit(picks, dtype, width, digit, row_count, densities, tensor):
    rows = tensor.shape[0]
    step = largest_step(width, 512, 128)
    slots = len(picks) * width // step
    smem = pl.BlockSpec(memory_space=pltpu.SMEM)
    vmem = pl.BlockSpec(memory_space=pltpu.VMEM)
    return pl.pallas_call(
        functools.partial(fit_kernel, picks, step),
        out_shape=[jax.ShapeDtypeStruct((densities.shape[0], width), dtype) for _ in picks],
        in_specs=[smem, smem, vmem, pl.BlockSpec(memory_space=pltpu.HBM)],
        out_specs=[vmem for _ in picks],
        scratch_shapes=[
            pltpu.VMEM((slots, rows, step), BF16),
            pltpu.SemaphoreType.DMA((slots,)),
        ],
        compiler_params=params(slots * rows * step * 2),
        cost_estimate=pl.CostEstimate(
            flops=2 * 16 * rows * step * slots,
            bytes_accessed=slots * rows * step * 2,
            transcendentals=0,
        ),
    )(digit, row_count, densities, pltpu.with_memory_space_constraint(tensor, pltpu.HBM))


def solve_kernel(picks, step, begun, digit_ref, metric_ref, *rest):
    fitted, rest = rest[: len(picks)], rest[len(picks) :]
    if begun:
        start_ref, rest = rest[0], rest[1:]
    out_ref, held, sems = rest
    depth = fitted[0].shape[1]
    copies = []
    for at, pick in enumerate(picks):
        first = (digit_ref[0] ^ pick) * depth
        for j in range(depth // step):
            slot = at * (depth // step) + j
            copy = pltpu.make_async_copy(
                metric_ref.at[pl.ds(pl.multiple_of(first + j * step, 128), step), :],
                held.at[slot],
                sems.at[slot],
            )
            copy.start()
            copies.append(copy)
    total = start_ref[...] if begun else jnp.zeros(out_ref.shape, F32)
    for at in range(len(picks)):
        for j in range(depth // step):
            slot = at * (depth // step) + j
            copies[slot].wait()
            total += jnp.dot(
                fitted[at][:, j * step : (j + 1) * step], held[slot], preferred_element_type=F32
            )
    out_ref[...] = total


def solve(picks, digit, metric, fitted, begun=None):
    depth, width = fitted[0].shape[1], metric.shape[1]
    step = largest_step(depth, 512, 128)
    slots = len(picks) * depth // step
    smem = pl.BlockSpec(memory_space=pltpu.SMEM)
    vmem = pl.BlockSpec(memory_space=pltpu.VMEM)
    extra = [] if begun is None else [begun]
    return pl.pallas_call(
        functools.partial(solve_kernel, picks, step, begun is not None),
        out_shape=jax.ShapeDtypeStruct((fitted[0].shape[0], width), F32),
        in_specs=[smem, pl.BlockSpec(memory_space=pltpu.HBM)] + [vmem] * (len(picks) + len(extra)),
        out_specs=vmem,
        scratch_shapes=[
            pltpu.VMEM((slots, step, width), BF16),
            pltpu.SemaphoreType.DMA((slots,)),
        ],
        compiler_params=params(slots * step * width * 2),
        cost_estimate=pl.CostEstimate(
            flops=2 * 16 * width * step * slots,
            bytes_accessed=slots * step * width * 2,
            transcendentals=0,
        ),
    )(digit, pltpu.with_memory_space_constraint(metric, pltpu.HBM), *fitted, *extra)


def back_kernel(step, begun, starts_ref, tensor_ref, pieces_ref, *rest):
    if begun:
        start_ref, rest = rest[0], rest[1:]
    out_ref, held, sems = rest
    count, _, width = pieces_ref.shape
    per = width // step
    copies = []
    for i in range(count):
        for j in range(per):
            copy = pltpu.make_async_copy(
                tensor_ref.at[:, pl.ds(pl.multiple_of(starts_ref[i] + j * step, 128), step)],
                held.at[i * per + j],
                sems.at[i * per + j],
            )
            copy.start()
            copies.append(copy)
    total = start_ref[...] if begun else jnp.zeros(out_ref.shape, F32)
    for i in range(count):
        for j in range(per):
            copies[i * per + j].wait()
            total += lax.dot_general(
                pieces_ref[i, :, j * step : (j + 1) * step],
                held[i * per + j],
                (((1,), (1,)), ((), ())),
                preferred_element_type=F32,
            )
    out_ref[...] = total


def back(starts, tensor, pieces, begun=None):
    rows = tensor.shape[0]
    count, k, width = pieces.shape
    step = largest_step(width, 640, 128)
    slots = count * width // step
    smem = pl.BlockSpec(memory_space=pltpu.SMEM)
    vmem = pl.BlockSpec(memory_space=pltpu.VMEM)
    extra = [] if begun is None else [begun]
    return pl.pallas_call(
        functools.partial(back_kernel, step, begun is not None),
        out_shape=jax.ShapeDtypeStruct((k, rows), F32),
        in_specs=[smem, pl.BlockSpec(memory_space=pltpu.HBM), vmem] + [vmem] * len(extra),
        out_specs=vmem,
        scratch_shapes=[
            pltpu.VMEM((slots, rows, step), BF16),
            pltpu.SemaphoreType.DMA((slots,)),
        ],
        compiler_params=params(slots * rows * step * 2),
        cost_estimate=pl.CostEstimate(
            flops=2 * 16 * rows * step * slots,
            bytes_accessed=slots * rows * step * 2,
            transcendentals=0,
        ),
    )(starts, pltpu.with_memory_space_constraint(tensor, pltpu.HBM), pieces, *extra)


def body(n_pairs, densities, tensor, metric, row_count):
    rows, half_aux = tensor.shape
    block = metric.shape[1]
    sizes = digits_of(n_pairs)
    me = lax.axis_index("pairs")
    core = lax.axis_index("aux")
    first, rest = sizes[0], sizes[1:]
    digit = (me % first).astype(jnp.int32).reshape(1)
    width = half_aux // first

    others = list(range(first - 1, 0, -1))
    sent = fit(others, BF16, width, digit, row_count, densities, tensor)
    arrived = [swap(x, "pairs", n_pairs, pick) for x, pick in zip(sent, others)]
    (total,) = fit([0], F32, width, digit, row_count, densities, tensor)
    for x in arrived:
        total = total + x.astype(F32)
    stride = first
    for size in rest:
        sending = total.astype(BF16)
        arrived = [swap(sending, "pairs", n_pairs, pick * stride) for pick in range(1, size)]
        for x in arrived:
            total = total + x.astype(F32)
        stride *= size
    fitted = total.astype(BF16)

    gathered = [swap(fitted, "pairs", n_pairs, pick) for pick in others]
    part = solve([0], digit, metric, [fitted])
    part = solve(others, digit, metric, gathered, part)

    half = block // 2
    keep = lax.dynamic_slice_in_dim(part, core * half, half, 1)
    give = lax.dynamic_slice_in_dim(part, (1 - core) * half, half, 1)
    piece = (keep + swap(give, "aux", 2, 1)).astype(BF16)

    last = sizes[-1]
    low = n_pairs // last
    mine = me // low
    got = []
    for pick in range(last):
        pairs = []
        for line in range(low):
            for high in range(last):
                a, i = high // (last // 2), high % (last // 2)
                for c in range(2):
                    to = (2 * i + c) ^ pick
                    pairs.append(((high * low + line) * 2 + c, (to * low + line) * 2 + a))
        got.append(lax.ppermute(piece, ("pairs", "aux"), pairs))
    held = jnp.stack(got)
    order = [mine ^ pick for pick in range(last)]
    origin = jnp.stack([(o // 2) * low * block + (o % 2) * half for o in order])

    line = me % low
    pieces, starts = held, origin + line * block
    if half % 128 == 0 and len(sizes) == 2:
        arrived = [swap(held, "pairs", n_pairs, pick) for pick in others]
        begun = back(starts.astype(jnp.int32), tensor, held)
        pieces = jnp.concatenate(arrived)
        starts = jnp.concatenate([origin + (line ^ pick) * block for pick in others])
        returned = back(starts.astype(jnp.int32), tensor, pieces, begun)
    else:
        stride = 1
        lines = [line]
        pieces = held[None]
        for size in sizes[:-1]:
            arrived = [pieces] + [swap(pieces, "pairs", n_pairs, pick * stride) for pick in range(1, size)]
            lines = [x ^ (pick * stride) for pick in range(size) for x in lines]
            pieces = jnp.concatenate(arrived)
            stride *= size
        whole = jnp.zeros((densities.shape[0], half_aux), BF16)
        for at, x in enumerate(lines):
            for pick in range(last):
                whole = lax.dynamic_update_slice_in_dim(
                    whole, pieces[at, pick], origin[pick] + x * block, 1
                )
        step = largest_step(half_aux, 640, 128)
        count = half_aux // step
        pieces = whole.reshape(-1, count, step).transpose(1, 0, 2)
        returned = back(jnp.arange(count, dtype=jnp.int32) * step, tensor, pieces)

    k_half = densities.shape[0] // 2
    keep = lax.dynamic_slice_in_dim(returned, core * k_half, k_half, 0)
    give = lax.dynamic_slice_in_dim(returned, (1 - core) * k_half, k_half, 0)
    coulomb = keep + swap(give, "aux", 2, 1)
    live = lax.broadcasted_iota(jnp.int32, (1, rows), 1) < row_count[0]
    return jnp.where(live, coulomb, 0.0).astype(BF16)


def solution(mesh):
    placed = (P(None, "pairs"), P("pairs", "aux"), P("aux", "pairs"), P("pairs"))
    return jax.shard_map(
        functools.partial(body, mesh.shape["pairs"]),
        mesh=mesh,
        in_specs=placed,
        out_specs=P("aux", "pairs"),
        check_vma=False,
    )
```

```python
import functools

import jax
import jax.numpy as jnp
from jax import lax
from jax.experimental import pallas as pl
from jax.experimental.pallas import tpu as pltpu
from jax.sharding import PartitionSpec as P

F32, BF16 = jnp.float32, jnp.bfloat16
MIB = 1 << 20


def digits_of(count):
    sizes = []
    while count > 1:
        size = 4 if count % 4 == 0 else 2
        sizes.append(size)
        count //= size
    return sizes


def largest_step(extent, limit, unit):
    return max(s for s in range(unit, limit + 1, unit) if extent % s == 0)


def swap(x, axis, count, mask):
    return lax.ppermute(x, axis, [(i, i ^ mask) for i in range(count)])


def params(used_bytes):
    return pltpu.CompilerParams(vmem_limit_bytes=used_bytes + 4 * MIB)


def in_hbm(x):
    return pltpu.with_memory_space_constraint(x, pltpu.HBM)


def in_vmem(x):
    return pltpu.with_memory_space_constraint(x, pltpu.VMEM)


def spec(space):
    return pl.BlockSpec(memory_space=space)


SMEM, VMEM, HBM = pltpu.SMEM, pltpu.VMEM, pltpu.HBM


def cost(flops, read):
    return pl.CostEstimate(flops=flops, bytes_accessed=read, transcendentals=0)


def slot_copies(digit, picks, per, tensor_ref, slots_ref, sems):
    step = slots_ref.shape[2]
    copies = []
    for at, pick in enumerate(picks):
        for j in range(per):
            slot = (digit ^ pick) * per + j
            copy = pltpu.make_async_copy(
                tensor_ref.at[:, pl.ds(pl.multiple_of(slot * step, 128), step)],
                slots_ref.at[slot],
                sems.at[at * per + j],
            )
            copy.start()
            copies.append((copy, slot))
    return copies


def fit_terms(masked, copies, per, slots_ref, outs):
    step = slots_ref.shape[2]
    for i, (copy, slot) in enumerate(copies):
        copy.wait()
        term = jnp.dot(masked, slots_ref[slot], preferred_element_type=F32)
        out, j = outs[i // per], i % per
        out[:, j * step : (j + 1) * step] = term.astype(out.dtype)


def fit_others_kernel(picks, per, info_ref, dens_hbm, tensor_ref, *rest):
    outs, (masked_ref, slots_ref, dens_ref, dens_sem, sems) = rest[: len(picks)], rest[len(picks) :]
    first = pltpu.make_async_copy(dens_hbm, dens_ref, dens_sem)
    first.start()
    copies = slot_copies(info_ref[0] & len(picks), picks, per, tensor_ref, slots_ref, sems)
    first.wait()
    dens = dens_ref[...]
    live = lax.broadcasted_iota(jnp.int32, dens.shape, 1) < info_ref[2]
    masked = jnp.where(live, dens.astype(F32), 0.0).astype(BF16)
    masked_ref[...] = masked
    fit_terms(masked, copies, per, slots_ref, outs)


def fit_others(picks, per, step, info, densities, tensor):
    rows, half_aux = tensor.shape
    k = densities.shape[0]
    n = len(picks) * per
    return pl.pallas_call(
        functools.partial(fit_others_kernel, picks, per),
        out_shape=[jax.ShapeDtypeStruct((k, per * step), BF16) for _ in picks]
        + [jax.ShapeDtypeStruct((k, rows), BF16), VMEM((half_aux // step, rows, step), BF16)],
        in_specs=[spec(SMEM), spec(HBM), spec(HBM)],
        out_specs=[spec(VMEM) for _ in range(len(picks) + 2)],
        scratch_shapes=[
            VMEM((k, rows), BF16),
            pltpu.SemaphoreType.DMA,
            pltpu.SemaphoreType.DMA((n,)),
        ],
        compiler_params=params(0),
        cost_estimate=cost(2 * k * rows * step * n, n * rows * step * 2),
    )(info, in_hbm(densities), in_hbm(tensor))


def row_copies(digit, picks, metric_ref, held, sems):
    depth = held[0].shape[0]
    copies = []
    for at, pick in enumerate(picks):
        first = pl.multiple_of((digit ^ pick) * depth, 128)
        copy = pltpu.make_async_copy(metric_ref.at[pl.ds(first, depth), :], held[at], sems.at[at])
        copy.start()
        copies.append(copy)
    return copies


def fit_own_kernel(
    per, top, info_ref, masked_ref, tensor_ref, metric_ref, before_ref, *rest
):
    out_ref, slots_ref, held_ref, sems, row_sems = rest
    digit = info_ref[0] & top
    copies = slot_copies(digit, [0], per, tensor_ref, slots_ref, sems)
    (rows_in,) = row_copies(digit, [0], metric_ref, [held_ref], row_sems)
    fit_terms(masked_ref[...], copies, per, slots_ref, [out_ref])
    rows_in.wait()


def fit_own(per, top, step, info, masked, tensor, metric, slots):
    rows = tensor.shape[0]
    k = masked.shape[0]
    depth, width = per * step, metric.shape[1]
    return pl.pallas_call(
        functools.partial(fit_own_kernel, per, top),
        out_shape=[
            jax.ShapeDtypeStruct((k, per * step), F32),
            VMEM(slots.shape, BF16),
            VMEM((depth, width), BF16),
        ],
        in_specs=[spec(SMEM), spec(VMEM), spec(HBM), spec(HBM), spec(VMEM)],
        out_specs=[spec(VMEM) for _ in range(3)],
        scratch_shapes=[pltpu.SemaphoreType.DMA((per,)), pltpu.SemaphoreType.DMA((1,))],
        input_output_aliases={4: 1},
        compiler_params=params(0),
        cost_estimate=cost(2 * k * rows * step * per, (per * rows * step + depth * width) * 2),
    )(info, masked, in_hbm(tensor), in_hbm(metric), in_vmem(slots))


def fetch_kernel(picks, top, info_ref, metric_ref, own_ref, *rest):
    *held, same_ref, sems = rest
    copies = row_copies(info_ref[0] & top, picks, metric_ref, held, sems)
    same_ref[...] = own_ref[...]
    for copy in copies:
        copy.wait()


def fetch(picks, top, depth, info, metric, own):
    width = metric.shape[1]
    return pl.pallas_call(
        functools.partial(fetch_kernel, picks, top),
        out_shape=[VMEM((depth, width), BF16) for _ in picks]
        + [jax.ShapeDtypeStruct(own.shape, own.dtype)],
        in_specs=[spec(SMEM), spec(HBM), spec(VMEM)],
        out_specs=[spec(VMEM) for _ in range(len(picks) + 1)],
        scratch_shapes=[pltpu.SemaphoreType.DMA((len(picks),))],
        compiler_params=params(0),
        cost_estimate=cost(0, len(picks) * depth * width * 2),
    )(info, in_hbm(metric), own)


def solve_own_kernel(
    picks, top, info_ref, metric_ref, fitted_ref, held_ref, out_ref, *rest
):
    *late, sems = rest
    copies = row_copies(info_ref[0] & top, picks, metric_ref, late, sems)
    out_ref[...] = jnp.dot(fitted_ref[...], held_ref[...], preferred_element_type=F32)
    for copy in copies:
        copy.wait()


def solve_own(picks, top, info, metric, fitted, held):
    k, depth = fitted.shape
    width = metric.shape[1]
    return pl.pallas_call(
        functools.partial(solve_own_kernel, picks, top),
        out_shape=[jax.ShapeDtypeStruct((k, width), F32)]
        + [VMEM((depth, width), BF16) for _ in picks],
        in_specs=[spec(SMEM), spec(HBM), spec(VMEM), spec(VMEM)],
        out_specs=[spec(VMEM) for _ in range(len(picks) + 1)],
        scratch_shapes=[pltpu.SemaphoreType.DMA((len(picks),))],
        compiler_params=params(0),
        cost_estimate=cost(2 * k * depth * width, (1 + len(picks)) * depth * width * 2),
    )(info, in_hbm(metric), fitted, in_vmem(held))


def solve_others_kernel(count, low, info_ref, begun_ref, *rest):
    fitted, held, (out_ref, home_ref) = rest[:count], rest[count : 2 * count], rest[2 * count :]
    total = begun_ref[...]
    for x, rows in zip(fitted, held):
        total += jnp.dot(x[...], rows[...], preferred_element_type=F32)
    out_ref[...] = total
    home = info_ref[0] >> (low.bit_length()) == info_ref[1]
    home_ref[...] = jnp.where(home, total, 0.0)


def solve_others(low, info, begun, fitted, held):
    k, depth = fitted[0].shape
    width = held[0].shape[1]
    count = len(fitted)
    return pl.pallas_call(
        functools.partial(solve_others_kernel, count, low),
        out_shape=[VMEM((k, width), F32) for _ in range(2)],
        in_specs=[spec(SMEM)] + [spec(VMEM) for _ in range(1 + 2 * count)],
        out_specs=[spec(VMEM), spec(VMEM)],
        compiler_params=params(0),
        cost_estimate=cost(2 * k * depth * width * count, count * depth * width * 2),
    )(info, begun, *fitted, *[in_vmem(x) for x in held])


def split_for_cores(total, axis, core, outs):
    if len(outs) == 1:
        outs[0][...] = total
        return
    low, high = jnp.split(total, 2, axis)
    outs[0][...] = jnp.where(core == 0, low, high)
    outs[1][...] = jnp.where(core == 0, high, low)


def back_kernel(which, begun, low, info_ref, slots_ref, *rest):
    pieces, rest = rest[: len(which)], rest[len(which) :]
    if begun:
        start_ref, *outs = rest
        total = start_ref[...]
    else:
        outs = rest
        total = jnp.zeros((pieces[0].shape[1], slots_ref.shape[1]), F32)
    line, mine = info_ref[0] & (low - 1), info_ref[0] >> (low.bit_length() - 1)
    step = slots_ref.shape[2]
    for part, place in zip(pieces, which):
        per = part.shape[2] // step
        for i in range(part.shape[0]):
            for j in range(per):
                slot = i
                if place is not None:
                    slot = (((mine ^ i) & 1) * low + (line ^ place)) * per + j
                total += lax.dot_general(
                    part[i, :, j * step : (j + 1) * step],
                    slots_ref[slot],
                    (((1,), (1,)), ((), ())),
                    preferred_element_type=F32,
                )
    split_for_cores(total, 0, info_ref[1], outs)


def back(which, low, info, slots, pieces, begun=None, split=True):
    rows = slots.shape[1]
    _, k, width = pieces[0].shape
    count = sum(part.shape[0] for part in pieces)
    extra = [] if begun is None else [begun]
    shapes = [(k // 2, rows)] * 2 if split else [(k, rows)]
    return pl.pallas_call(
        functools.partial(back_kernel, which, begun is not None, low),
        out_shape=[jax.ShapeDtypeStruct(shape, F32) for shape in shapes],
        in_specs=[spec(SMEM), spec(VMEM)] + [spec(VMEM) for _ in pieces + extra],
        out_specs=[spec(VMEM) for _ in shapes],
        compiler_params=params(0),
        cost_estimate=cost(2 * k * rows * width * count, count * rows * width * 2),
    )(info, in_vmem(slots), *pieces, *extra)


def body(n_pairs, densities, tensor, metric, row_count):
    rows, half_aux = tensor.shape
    block = metric.shape[1]
    sizes = digits_of(n_pairs)
    me = lax.axis_index("pairs")
    core = lax.axis_index("aux")
    first, rest = sizes[0], sizes[1:]
    info = jnp.stack([me.astype(jnp.int32), core.astype(jnp.int32), row_count[0]])
    width = half_aux // first

    others = list(range(first - 1, 0, -1))
    step = largest_step(width, 640, 128)
    per = width // step
    *sent, masked, slots = fit_others(others, per, step, info, densities, tensor)
    arrived = [swap(x, "pairs", n_pairs, pick) for x, pick in zip(sent, others)]
    total, slots, held = fit_own(per, first - 1, step, info, masked, tensor, metric, slots)
    for x in arrived:
        total = total + x.astype(F32)
    here = len(others) - 1
    stride = first
    for size in rest:
        sending = total.astype(BF16)
        arrived = [swap(sending, "pairs", n_pairs, pick * stride) for pick in range(1, size)]
        if stride == first:
            *rows_of, total = fetch(others[:here], first - 1, width, info, metric, total)
        for x in arrived:
            total = total + x.astype(F32)
        stride *= size
    fitted = total.astype(BF16)

    gathered = [swap(fitted, "pairs", n_pairs, pick) for pick in others]
    part, *late = solve_own(others[here:], first - 1, info, metric, fitted, held)
    last = sizes[-1]
    low = n_pairs // last
    part, at_home = solve_others(low, info, part, gathered, rows_of + late)

    homes = [(p, (p // low) // 2) for p in range(n_pairs)]
    across = 2 * low

    def send(x, pairs):
        return lax.ppermute(x, ("pairs", "aux"), [(p * 2 + c, q * 2 + d) for p, c, q, d in pairs])

    term = part.astype(BF16)
    first_pairs = [(p, 1 - c, p, c) for p, c in homes] + [(p, c, p ^ across, c) for p, c in homes]
    other_term = send(term, first_pairs)
    third_term = send(term, [(p, 1 - c, p ^ across, c) for p, c in homes])
    own = (at_home + other_term.astype(F32) + third_term.astype(F32)).astype(BF16)
    line_blocks = jnp.stack([own, swap(own, "pairs", n_pairs, low)])

    if block % step == 0 and len(sizes) == 2:
        arrived = [swap(line_blocks, "pairs", n_pairs, pick) for pick in others]
        (begun,) = back([0], low, info, slots, [line_blocks], split=False)
        (begun,) = back(others[:1], low, info, slots, arrived[:1], begun, split=False)
        keep, give = back(others[1:], low, info, slots, arrived[1:], begun)
    else:
        mine = me // low
        origin = [((mine ^ i) & 1) * low * block for i in range(2)]
        stride = 1
        lines = [me % low]
        pieces = line_blocks[None]
        for size in sizes[:-1]:
            arrived = [pieces] + [swap(pieces, "pairs", n_pairs, pick * stride) for pick in range(1, size)]
            lines = [x ^ (pick * stride) for pick in range(size) for x in lines]
            pieces = jnp.concatenate(arrived)
            stride *= size
        whole = jnp.zeros((densities.shape[0], half_aux), BF16)
        for at, x in enumerate(lines):
            for i in range(2):
                whole = lax.dynamic_update_slice_in_dim(
                    whole, pieces[at, i], origin[i] + x * block, 1
                )
        count = half_aux // step
        pieces = whole.reshape(-1, count, step).transpose(1, 0, 2)
        keep, give = back([None], low, info, slots, [pieces])

    coulomb = keep + swap(give, "aux", 2, 1)
    live = lax.broadcasted_iota(jnp.int32, (1, rows), 1) < row_count[0]
    return jnp.where(live, coulomb, 0.0).astype(BF16)


def solution(mesh):
    placed = (P(None, "pairs"), P("pairs", "aux"), P("aux", "pairs"), P("pairs"))
    return jax.shard_map(
        functools.partial(body, mesh.shape["pairs"]),
        mesh=mesh,
        in_specs=placed,
        out_specs=P("aux", "pairs"),
        check_vma=False,
    )
```

```python
import functools

import jax
import jax.numpy as jnp
from jax import lax
from jax.experimental import pallas as pl
from jax.experimental.pallas import tpu as pltpu
from jax.sharding import PartitionSpec as P

F32, BF16 = jnp.float32, jnp.bfloat16
MIB = 1 << 20


def digits_of(count):
    sizes = []
    while count > 1:
        size = 4 if count % 4 == 0 else 2
        sizes.append(size)
        count //= size
    return sizes


def largest_step(extent, limit, unit):
    return max(s for s in range(unit, limit + 1, unit) if extent % s == 0)


def swap(x, axis, count, mask):
    return lax.ppermute(x, axis, [(i, i ^ mask) for i in range(count)])


def params(used_bytes):
    return pltpu.CompilerParams(vmem_limit_bytes=used_bytes + 4 * MIB)


def in_hbm(x):
    return pltpu.with_memory_space_constraint(x, pltpu.HBM)


def in_vmem(x):
    return pltpu.with_memory_space_constraint(x, pltpu.VMEM)


def spec(space):
    return pl.BlockSpec(memory_space=space)


VMEM, HBM = pltpu.VMEM, pltpu.HBM


def field(info_ref, at):
    return info_ref[...][0, at]


def cost(flops, read):
    return pl.CostEstimate(flops=flops, bytes_accessed=read, transcendentals=0)


def slot_copies(digit, picks, per, tensor_ref, slots_ref, sems):
    step = slots_ref.shape[2]
    copies = []
    for at, pick in enumerate(picks):
        for j in range(per):
            slot = (digit ^ pick) * per + j
            copy = pltpu.make_async_copy(
                tensor_ref.at[:, pl.ds(pl.multiple_of(slot * step, 128), step)],
                slots_ref.at[slot],
                sems.at[at * per + j],
            )
            copy.start()
            copies.append((copy, slot))
    return copies


def fit_terms(masked, copies, per, slots_ref, outs):
    step = slots_ref.shape[2]
    for i, (copy, slot) in enumerate(copies):
        copy.wait()
        term = jnp.dot(masked, slots_ref[slot], preferred_element_type=F32)
        out, j = outs[i // per], i % per
        out[:, j * step : (j + 1) * step] = term.astype(out.dtype)


def fit_others_kernel(picks, per, info_ref, dens_hbm, tensor_ref, *rest):
    outs, (masked_ref, slots_ref, dens_ref, dens_sem, sems) = rest[: len(picks)], rest[len(picks) :]
    first = pltpu.make_async_copy(dens_hbm, dens_ref, dens_sem)
    first.start()
    copies = slot_copies(field(info_ref, 0) & len(picks), picks, per, tensor_ref, slots_ref, sems)
    first.wait()
    dens = dens_ref[...]
    live = lax.broadcasted_iota(jnp.int32, dens.shape, 1) < field(info_ref, 2)
    masked = jnp.where(live, dens.astype(F32), 0.0).astype(BF16)
    masked_ref[...] = masked
    fit_terms(masked, copies, per, slots_ref, outs)


def fit_others(picks, per, step, info, densities, tensor):
    rows, half_aux = tensor.shape
    k = densities.shape[0]
    n = len(picks) * per
    return pl.pallas_call(
        functools.partial(fit_others_kernel, picks, per),
        out_shape=[jax.ShapeDtypeStruct((k, per * step), BF16) for _ in picks]
        + [jax.ShapeDtypeStruct((k, rows), BF16), VMEM((half_aux // step, rows, step), BF16)],
        in_specs=[spec(VMEM), spec(HBM), spec(HBM)],
        out_specs=[spec(VMEM) for _ in range(len(picks) + 2)],
        scratch_shapes=[
            VMEM((k, rows), BF16),
            pltpu.SemaphoreType.DMA,
            pltpu.SemaphoreType.DMA((n,)),
        ],
        compiler_params=params(0),
        cost_estimate=cost(2 * k * rows * step * n, n * rows * step * 2),
    )(info, in_hbm(densities), in_hbm(tensor))


def row_copies(digit, picks, metric_ref, held, sems):
    depth = held[0].shape[0]
    copies = []
    for at, pick in enumerate(picks):
        first = pl.multiple_of((digit ^ pick) * depth, 128)
        copy = pltpu.make_async_copy(metric_ref.at[pl.ds(first, depth), :], held[at], sems.at[at])
        copy.start()
        copies.append(copy)
    return copies


def fit_own_kernel(
    per, top, info_ref, masked_ref, tensor_ref, metric_ref, before_ref, *rest
):
    out_ref, slots_ref, held_ref, sems, row_sems = rest
    digit = field(info_ref, 0) & top
    copies = slot_copies(digit, [0], per, tensor_ref, slots_ref, sems)
    (rows_in,) = row_copies(digit, [0], metric_ref, [held_ref], row_sems)
    fit_terms(masked_ref[...], copies, per, slots_ref, [out_ref])
    rows_in.wait()


def fit_own(per, top, step, info, masked, tensor, metric, slots):
    rows = tensor.shape[0]
    k = masked.shape[0]
    depth, width = per * step, metric.shape[1]
    return pl.pallas_call(
        functools.partial(fit_own_kernel, per, top),
        out_shape=[
            jax.ShapeDtypeStruct((k, per * step), F32),
            VMEM(slots.shape, BF16),
            VMEM((depth, width), BF16),
        ],
        in_specs=[spec(VMEM), spec(VMEM), spec(HBM), spec(HBM), spec(VMEM)],
        out_specs=[spec(VMEM) for _ in range(3)],
        scratch_shapes=[pltpu.SemaphoreType.DMA((per,)), pltpu.SemaphoreType.DMA((1,))],
        input_output_aliases={4: 1},
        compiler_params=params(0),
        cost_estimate=cost(2 * k * rows * step * per, (per * rows * step + depth * width) * 2),
    )(info, masked, in_hbm(tensor), in_hbm(metric), in_vmem(slots))


def fetch_kernel(picks, top, info_ref, metric_ref, own_ref, *rest):
    *held, same_ref, sems = rest
    copies = row_copies(field(info_ref, 0) & top, picks, metric_ref, held, sems)
    same_ref[...] = own_ref[...]
    for copy in copies:
        copy.wait()


def fetch(picks, top, depth, info, metric, own):
    width = metric.shape[1]
    return pl.pallas_call(
        functools.partial(fetch_kernel, picks, top),
        out_shape=[VMEM((depth, width), BF16) for _ in picks]
        + [jax.ShapeDtypeStruct(own.shape, own.dtype)],
        in_specs=[spec(VMEM), spec(HBM), spec(VMEM)],
        out_specs=[spec(VMEM) for _ in range(len(picks) + 1)],
        scratch_shapes=[pltpu.SemaphoreType.DMA((len(picks),))],
        compiler_params=params(0),
        cost_estimate=cost(0, len(picks) * depth * width * 2),
    )(info, in_hbm(metric), own)


def solve_own_kernel(
    picks, top, info_ref, metric_ref, fitted_ref, held_ref, out_ref, *rest
):
    *late, sems = rest
    copies = row_copies(field(info_ref, 0) & top, picks, metric_ref, late, sems)
    out_ref[...] = jnp.dot(fitted_ref[...], held_ref[...], preferred_element_type=F32)
    for copy in copies:
        copy.wait()


def solve_own(picks, top, info, metric, fitted, held):
    k, depth = fitted.shape
    width = metric.shape[1]
    return pl.pallas_call(
        functools.partial(solve_own_kernel, picks, top),
        out_shape=[jax.ShapeDtypeStruct((k, width), F32)]
        + [VMEM((depth, width), BF16) for _ in picks],
        in_specs=[spec(VMEM), spec(HBM), spec(VMEM), spec(VMEM)],
        out_specs=[spec(VMEM) for _ in range(len(picks) + 1)],
        scratch_shapes=[pltpu.SemaphoreType.DMA((len(picks),))],
        compiler_params=params(0),
        cost_estimate=cost(2 * k * depth * width, (1 + len(picks)) * depth * width * 2),
    )(info, in_hbm(metric), fitted, in_vmem(held))


def solve_others_kernel(count, low, info_ref, begun_ref, *rest):
    fitted, held, (out_ref, home_ref) = rest[:count], rest[count : 2 * count], rest[2 * count :]
    total = begun_ref[...]
    for x, rows in zip(fitted, held):
        total += jnp.dot(x[...], rows[...], preferred_element_type=F32)
    out_ref[...] = total
    home = field(info_ref, 0) >> (low.bit_length()) == field(info_ref, 1)
    home_ref[...] = jnp.where(home, total, 0.0)


def solve_others(low, info, begun, fitted, held):
    k, depth = fitted[0].shape
    width = held[0].shape[1]
    count = len(fitted)
    return pl.pallas_call(
        functools.partial(solve_others_kernel, count, low),
        out_shape=[VMEM((k, width), F32) for _ in range(2)],
        in_specs=[spec(VMEM)] + [spec(VMEM) for _ in range(1 + 2 * count)],
        out_specs=[spec(VMEM), spec(VMEM)],
        compiler_params=params(0),
        cost_estimate=cost(2 * k * depth * width * count, count * depth * width * 2),
    )(info, begun, *fitted, *[in_vmem(x) for x in held])


def split_for_cores(total, axis, core, outs):
    if len(outs) == 1:
        outs[0][...] = total
        return
    low, high = jnp.split(total, 2, axis)
    outs[0][...] = jnp.where(core == 0, low, high)
    outs[1][...] = jnp.where(core == 0, high, low)


def back_kernel(which, begun, low, info_ref, slots_ref, *rest):
    pieces, rest = rest[: len(which)], rest[len(which) :]
    if begun:
        start_ref, *outs = rest
        total = start_ref[...]
    else:
        outs = rest
        total = jnp.zeros((pieces[0].shape[1], slots_ref.shape[1]), F32)
    line, mine = field(info_ref, 0) & (low - 1), field(info_ref, 0) >> (low.bit_length() - 1)
    step = slots_ref.shape[2]
    for part, place in zip(pieces, which):
        per = part.shape[2] // step
        for i in range(part.shape[0]):
            for j in range(per):
                slot = i
                if place is not None:
                    slot = (((mine ^ i) & 1) * low + (line ^ place)) * per + j
                total += lax.dot_general(
                    part[i, :, j * step : (j + 1) * step],
                    slots_ref[slot],
                    (((1,), (1,)), ((), ())),
                    preferred_element_type=F32,
                )
    split_for_cores(total, 0, field(info_ref, 1), outs)


def back(which, low, info, slots, pieces, begun=None, split=True):
    rows = slots.shape[1]
    _, k, width = pieces[0].shape
    count = sum(part.shape[0] for part in pieces)
    extra = [] if begun is None else [begun]
    shapes = [(k // 2, rows)] * 2 if split else [(k, rows)]
    return pl.pallas_call(
        functools.partial(back_kernel, which, begun is not None, low),
        out_shape=[jax.ShapeDtypeStruct(shape, F32) for shape in shapes],
        in_specs=[spec(VMEM), spec(VMEM)] + [spec(VMEM) for _ in pieces + extra],
        out_specs=[spec(VMEM) for _ in shapes],
        compiler_params=params(0),
        cost_estimate=cost(2 * k * rows * width * count, count * rows * width * 2),
    )(info, in_vmem(slots), *pieces, *extra)


def body(n_pairs, densities, tensor, metric, row_count):
    rows, half_aux = tensor.shape
    block = metric.shape[1]
    sizes = digits_of(n_pairs)
    me = lax.axis_index("pairs")
    core = lax.axis_index("aux")
    first, rest = sizes[0], sizes[1:]
    info = jnp.stack([me.astype(jnp.int32), core.astype(jnp.int32), row_count[0]]).reshape(1, 3)
    width = half_aux // first

    others = list(range(first - 1, 0, -1))
    step = largest_step(width, 640, 128)
    per = width // step
    *sent, masked, slots = fit_others(others, per, step, info, densities, tensor)
    arrived = [swap(x, "pairs", n_pairs, pick) for x, pick in zip(sent, others)]
    total, slots, held = fit_own(per, first - 1, step, info, masked, tensor, metric, slots)
    for x in arrived:
        total = total + x.astype(F32)
    here = len(others) - 1
    stride = first
    for size in rest:
        sending = total.astype(BF16)
        arrived = [swap(sending, "pairs", n_pairs, pick * stride) for pick in range(1, size)]
        if stride == first:
            *rows_of, total = fetch(others[:here], first - 1, width, info, metric, total)
        for x in arrived:
            total = total + x.astype(F32)
        stride *= size
    fitted = total.astype(BF16)

    gathered = [swap(fitted, "pairs", n_pairs, pick) for pick in others]
    part, *late = solve_own(others[here:], first - 1, info, metric, fitted, held)
    last = sizes[-1]
    low = n_pairs // last
    part, at_home = solve_others(low, info, part, gathered, rows_of + late)

    homes = [(p, (p // low) // 2) for p in range(n_pairs)]
    across = 2 * low

    def send(x, pairs):
        return lax.ppermute(x, ("pairs", "aux"), [(p * 2 + c, q * 2 + d) for p, c, q, d in pairs])

    term = part.astype(BF16)
    first_pairs = [(p, 1 - c, p, c) for p, c in homes] + [(p, c, p ^ across, c) for p, c in homes]
    other_term = send(term, first_pairs)
    third_term = send(term, [(p, 1 - c, p ^ across, c) for p, c in homes])
    own = (at_home + other_term.astype(F32) + third_term.astype(F32)).astype(BF16)
    line_blocks = jnp.stack([own, swap(own, "pairs", n_pairs, low)])

    if block % step == 0 and len(sizes) == 2:
        arrived = [swap(line_blocks, "pairs", n_pairs, pick) for pick in others]
        (begun,) = back([0], low, info, slots, [line_blocks], split=False)
        (begun,) = back(others[:1], low, info, slots, arrived[:1], begun, split=False)
        keep, give = back(others[1:], low, info, slots, arrived[1:], begun)
    else:
        mine = me // low
        origin = [((mine ^ i) & 1) * low * block for i in range(2)]
        stride = 1
        lines = [me % low]
        pieces = line_blocks[None]
        for size in sizes[:-1]:
            arrived = [pieces] + [swap(pieces, "pairs", n_pairs, pick * stride) for pick in range(1, size)]
            lines = [x ^ (pick * stride) for pick in range(size) for x in lines]
            pieces = jnp.concatenate(arrived)
            stride *= size
        whole = jnp.zeros((densities.shape[0], half_aux), BF16)
        for at, x in enumerate(lines):
            for i in range(2):
                whole = lax.dynamic_update_slice_in_dim(
                    whole, pieces[at, i], origin[i] + x * block, 1
                )
        count = half_aux // step
        pieces = whole.reshape(-1, count, step).transpose(1, 0, 2)
        keep, give = back([None], low, info, slots, [pieces])

    coulomb = keep + swap(give, "aux", 2, 1)
    live = lax.broadcasted_iota(jnp.int32, (1, rows), 1) < row_count[0]
    return jnp.where(live, coulomb, 0.0).astype(BF16)


def solution(mesh):
    placed = (P(None, "pairs"), P("pairs", "aux"), P("aux", "pairs"), P("pairs"))
    return jax.shard_map(
        functools.partial(body, mesh.shape["pairs"]),
        mesh=mesh,
        in_specs=placed,
        out_specs=P("aux", "pairs"),
        check_vma=False,
    )
```

```python
import functools

import jax
import jax.numpy as jnp
from jax import lax
from jax.experimental import pallas as pl
from jax.experimental.pallas import tpu as pltpu
from jax.sharding import PartitionSpec as P

F32, BF16 = jnp.float32, jnp.bfloat16
MIB = 1 << 20


def digits_of(count):
    sizes = []
    while count > 1:
        size = 4 if count % 4 == 0 else 2
        sizes.append(size)
        count //= size
    return sizes


def largest_step(extent, limit, unit):
    return max(s for s in range(unit, limit + 1, unit) if extent % s == 0)


def swap(x, axis, count, mask):
    return lax.ppermute(x, axis, [(i, i ^ mask) for i in range(count)])


def params(used_bytes):
    return pltpu.CompilerParams(vmem_limit_bytes=used_bytes + 4 * MIB)


def in_hbm(x):
    return pltpu.with_memory_space_constraint(x, pltpu.HBM)


def in_vmem(x):
    return pltpu.with_memory_space_constraint(x, pltpu.VMEM)


def spec(space):
    return pl.BlockSpec(memory_space=space)


VMEM, HBM = pltpu.VMEM, pltpu.HBM


def field(info_ref, at):
    return info_ref[...][0, at]


def cost(flops, read):
    return pl.CostEstimate(flops=flops, bytes_accessed=read, transcendentals=0)


def slot_copies(digit, picks, per, tensor_ref, slots_ref, sems):
    step = slots_ref.shape[2]
    copies = []
    for at, pick in enumerate(picks):
        for j in range(per):
            slot = (digit ^ pick) * per + j
            copy = pltpu.make_async_copy(
                tensor_ref.at[:, pl.ds(pl.multiple_of(slot * step, 128), step)],
                slots_ref.at[slot],
                sems.at[at * per + j],
            )
            copy.start()
            copies.append((copy, slot))
    return copies


def fit_terms(masked, copies, per, slots_ref, outs):
    step = slots_ref.shape[2]
    for i, (copy, slot) in enumerate(copies):
        copy.wait()
        term = jnp.dot(masked, slots_ref[slot], preferred_element_type=F32)
        out, j = outs[i // per], i % per
        out[:, j * step : (j + 1) * step] = term.astype(out.dtype)


def fit_others_kernel(picks, per, info_ref, dens_hbm, tensor_ref, *rest):
    outs, (masked_ref, slots_ref, dens_ref, dens_sem, sems) = rest[: len(picks)], rest[len(picks) :]
    first = pltpu.make_async_copy(dens_hbm, dens_ref, dens_sem)
    first.start()
    copies = slot_copies(field(info_ref, 0) & len(picks), picks, per, tensor_ref, slots_ref, sems)
    first.wait()
    dens = dens_ref[...]
    live = lax.broadcasted_iota(jnp.int32, dens.shape, 1) < field(info_ref, 2)
    masked = jnp.where(live, dens.astype(F32), 0.0).astype(BF16)
    masked_ref[...] = masked
    fit_terms(masked, copies, per, slots_ref, outs)


def fit_others(picks, per, step, info, densities, tensor):
    rows, half_aux = tensor.shape
    k = densities.shape[0]
    n = len(picks) * per
    return pl.pallas_call(
        functools.partial(fit_others_kernel, picks, per),
        out_shape=[jax.ShapeDtypeStruct((k, per * step), BF16) for _ in picks]
        + [jax.ShapeDtypeStruct((k, rows), BF16), VMEM((half_aux // step, rows, step), BF16)],
        in_specs=[spec(VMEM), spec(HBM), spec(HBM)],
        out_specs=[spec(VMEM) for _ in range(len(picks) + 2)],
        scratch_shapes=[
            VMEM((k, rows), BF16),
            pltpu.SemaphoreType.DMA,
            pltpu.SemaphoreType.DMA((n,)),
        ],
        compiler_params=params(0),
        cost_estimate=cost(2 * k * rows * step * n, n * rows * step * 2),
    )(info, in_hbm(densities), in_hbm(tensor))


def row_copies(digit, picks, metric_ref, held, sems):
    depth = held[0].shape[0]
    copies = []
    for at, pick in enumerate(picks):
        first = pl.multiple_of((digit ^ pick) * depth, 128)
        copy = pltpu.make_async_copy(metric_ref.at[pl.ds(first, depth), :], held[at], sems.at[at])
        copy.start()
        copies.append(copy)
    return copies


def fit_own_kernel(
    per, top, info_ref, masked_ref, tensor_ref, metric_ref, before_ref, *rest
):
    out_ref, slots_ref, held_ref, sems, row_sems = rest
    digit = field(info_ref, 0) & top
    copies = slot_copies(digit, [0], per, tensor_ref, slots_ref, sems)
    (rows_in,) = row_copies(digit, [0], metric_ref, [held_ref], row_sems)
    fit_terms(masked_ref[...], copies, per, slots_ref, [out_ref])
    rows_in.wait()


def fit_own(per, top, step, info, masked, tensor, metric, slots):
    rows = tensor.shape[0]
    k = masked.shape[0]
    depth, width = per * step, metric.shape[1]
    return pl.pallas_call(
        functools.partial(fit_own_kernel, per, top),
        out_shape=[
            jax.ShapeDtypeStruct((k, per * step), F32),
            VMEM(slots.shape, BF16),
            VMEM((depth, width), BF16),
        ],
        in_specs=[spec(VMEM), spec(VMEM), spec(HBM), spec(HBM), spec(VMEM)],
        out_specs=[spec(VMEM) for _ in range(3)],
        scratch_shapes=[pltpu.SemaphoreType.DMA((per,)), pltpu.SemaphoreType.DMA((1,))],
        input_output_aliases={4: 1},
        compiler_params=params(0),
        cost_estimate=cost(2 * k * rows * step * per, (per * rows * step + depth * width) * 2),
    )(info, masked, in_hbm(tensor), in_hbm(metric), in_vmem(slots))


def fetch_kernel(picks, top, info_ref, metric_ref, own_ref, *rest):
    *held, same_ref, sems = rest
    copies = row_copies(field(info_ref, 0) & top, picks, metric_ref, held, sems)
    same_ref[...] = own_ref[...]
    for copy in copies:
        copy.wait()


def fetch(picks, top, depth, info, metric, own):
    width = metric.shape[1]
    return pl.pallas_call(
        functools.partial(fetch_kernel, picks, top),
        out_shape=[VMEM((depth, width), BF16) for _ in picks]
        + [jax.ShapeDtypeStruct(own.shape, own.dtype)],
        in_specs=[spec(VMEM), spec(HBM), spec(VMEM)],
        out_specs=[spec(VMEM) for _ in range(len(picks) + 1)],
        scratch_shapes=[pltpu.SemaphoreType.DMA((len(picks),))],
        compiler_params=params(0),
        cost_estimate=cost(0, len(picks) * depth * width * 2),
    )(info, in_hbm(metric), own)


def solve_own_kernel(
    picks, top, info_ref, metric_ref, fitted_ref, held_ref, out_ref, *rest
):
    *late, sems = rest
    copies = row_copies(field(info_ref, 0) & top, picks, metric_ref, late, sems)
    out_ref[...] = jnp.dot(fitted_ref[...], held_ref[...], preferred_element_type=F32)
    for copy in copies:
        copy.wait()


def solve_own(picks, top, info, metric, fitted, held):
    k, depth = fitted.shape
    width = metric.shape[1]
    return pl.pallas_call(
        functools.partial(solve_own_kernel, picks, top),
        out_shape=[jax.ShapeDtypeStruct((k, width), F32)]
        + [VMEM((depth, width), BF16) for _ in picks],
        in_specs=[spec(VMEM), spec(HBM), spec(VMEM), spec(VMEM)],
        out_specs=[spec(VMEM) for _ in range(len(picks) + 1)],
        scratch_shapes=[pltpu.SemaphoreType.DMA((len(picks),))],
        compiler_params=params(0),
        cost_estimate=cost(2 * k * depth * width, (1 + len(picks)) * depth * width * 2),
    )(info, in_hbm(metric), fitted, in_vmem(held))


def solve_others_kernel(count, low, info_ref, begun_ref, *rest):
    fitted, held, (out_ref, home_ref) = rest[:count], rest[count : 2 * count], rest[2 * count :]
    total = begun_ref[...]
    for x, rows in zip(fitted, held):
        total += jnp.dot(x[...], rows[...], preferred_element_type=F32)
    out_ref[...] = total
    home = field(info_ref, 0) >> (low.bit_length()) == field(info_ref, 1)
    home_ref[...] = jnp.where(home, total, 0.0)


def solve_others(low, info, begun, fitted, held):
    k, depth = fitted[0].shape
    width = held[0].shape[1]
    count = len(fitted)
    return pl.pallas_call(
        functools.partial(solve_others_kernel, count, low),
        out_shape=[VMEM((k, width), F32) for _ in range(2)],
        in_specs=[spec(VMEM)] + [spec(VMEM) for _ in range(1 + 2 * count)],
        out_specs=[spec(VMEM), spec(VMEM)],
        compiler_params=params(0),
        cost_estimate=cost(2 * k * depth * width * count, count * depth * width * 2),
    )(info, begun, *fitted, *[in_vmem(x) for x in held])


def split_for_cores(total, axis, core, outs):
    if len(outs) == 1:
        outs[0][...] = total
        return
    low, high = jnp.split(total, 2, axis)
    outs[0][...] = jnp.where(core == 0, low, high)
    outs[1][...] = jnp.where(core == 0, high, low)


def back_kernel(which, begun, low, info_ref, slots_ref, *rest):
    pieces, rest = rest[: len(which)], rest[len(which) :]
    if begun:
        start_ref, *outs = rest
        total = start_ref[...]
    else:
        outs = rest
        total = jnp.zeros((pieces[0].shape[1], slots_ref.shape[1]), F32)
    line, mine = field(info_ref, 0) & (low - 1), field(info_ref, 0) >> (low.bit_length() - 1)
    step = slots_ref.shape[2]
    for part, place in zip(pieces, which):
        per = part.shape[2] // step
        for i in range(part.shape[0]):
            for j in range(per):
                slot = i
                if place is not None:
                    slot = (((mine ^ i) & 1) * low + (line ^ place)) * per + j
                total += lax.dot_general(
                    part[i, :, j * step : (j + 1) * step],
                    slots_ref[slot],
                    (((1,), (1,)), ((), ())),
                    preferred_element_type=F32,
                )
    split_for_cores(total, 0, field(info_ref, 1), outs)


def back(which, low, info, slots, pieces, begun=None, split=True):
    rows = slots.shape[1]
    _, k, width = pieces[0].shape
    count = sum(part.shape[0] for part in pieces)
    extra = [] if begun is None else [begun]
    shapes = [(k // 2, rows)] * 2 if split else [(k, rows)]
    return pl.pallas_call(
        functools.partial(back_kernel, which, begun is not None, low),
        out_shape=[jax.ShapeDtypeStruct(shape, F32) for shape in shapes],
        in_specs=[spec(VMEM), spec(VMEM)] + [spec(VMEM) for _ in pieces + extra],
        out_specs=[spec(VMEM) for _ in shapes],
        compiler_params=params(0),
        cost_estimate=cost(2 * k * rows * width * count, count * rows * width * 2),
    )(info, in_vmem(slots), *pieces, *extra)


def body(n_pairs, densities, tensor, metric, row_count):
    rows, half_aux = tensor.shape
    block = metric.shape[1]
    sizes = digits_of(n_pairs)
    me = lax.axis_index("pairs")
    core = lax.axis_index("aux")
    first, rest = sizes[0], sizes[1:]
    info = jnp.stack([me.astype(jnp.int32), core.astype(jnp.int32), row_count[0]]).reshape(1, 3)
    width = half_aux // first

    others = list(range(first - 1, 0, -1))
    step = largest_step(width, 640, 128)
    per = width // step
    *sent, masked, slots = fit_others(others, per, step, info, densities, tensor)
    arrived = [swap(x, "pairs", n_pairs, pick) for x, pick in zip(sent, others)]
    total, slots, held = fit_own(per, first - 1, step, info, masked, tensor, metric, slots)
    for x in arrived:
        total = total + x.astype(F32)
    here = len(others) - 1
    stride = first
    for size in rest:
        sending = total.astype(BF16)
        arrived = [swap(sending, "pairs", n_pairs, pick * stride) for pick in range(1, size)]
        if stride == first:
            *rows_of, total = fetch(others[:here], first - 1, width, info, metric, total)
        for x in arrived:
            total = total + x.astype(F32)
        stride *= size
    fitted = total.astype(BF16)

    gathered = [swap(fitted, "pairs", n_pairs, pick) for pick in others]
    part, *late = solve_own(others[here:], first - 1, info, metric, fitted, held)
    last = sizes[-1]
    low = n_pairs // last
    part, at_home = solve_others(low, info, part, gathered, rows_of + late)

    homes = [(p, (p // low) // 2) for p in range(n_pairs)]
    across = 2 * low

    def send(x, pairs):
        return lax.ppermute(x, ("pairs", "aux"), [(p * 2 + c, q * 2 + d) for p, c, q, d in pairs])

    term = part.astype(BF16)
    first_pairs = [(p, 1 - c, p, c) for p, c in homes] + [(p, c, p ^ across, c) for p, c in homes]
    third_term = send(term, [(p, 1 - c, p ^ across, c) for p, c in homes])
    other_term = send(term, first_pairs)
    own = (at_home + third_term.astype(F32) + other_term.astype(F32)).astype(BF16)
    line_blocks = jnp.stack([own, swap(own, "pairs", n_pairs, low)])

    if block % step == 0 and len(sizes) == 2:
        arrived = [swap(line_blocks, "pairs", n_pairs, pick) for pick in others]
        (begun,) = back([0], low, info, slots, [line_blocks], split=False)
        (begun,) = back(others[:1], low, info, slots, arrived[:1], begun, split=False)
        keep, give = back(others[1:], low, info, slots, arrived[1:], begun)
    else:
        mine = me // low
        origin = [((mine ^ i) & 1) * low * block for i in range(2)]
        stride = 1
        lines = [me % low]
        pieces = line_blocks[None]
        for size in sizes[:-1]:
            arrived = [pieces] + [swap(pieces, "pairs", n_pairs, pick * stride) for pick in range(1, size)]
            lines = [x ^ (pick * stride) for pick in range(size) for x in lines]
            pieces = jnp.concatenate(arrived)
            stride *= size
        whole = jnp.zeros((densities.shape[0], half_aux), BF16)
        for at, x in enumerate(lines):
            for i in range(2):
                whole = lax.dynamic_update_slice_in_dim(
                    whole, pieces[at, i], origin[i] + x * block, 1
                )
        count = half_aux // step
        pieces = whole.reshape(-1, count, step).transpose(1, 0, 2)
        keep, give = back([None], low, info, slots, [pieces])

    coulomb = keep + swap(give, "aux", 2, 1)
    live = lax.broadcasted_iota(jnp.int32, (1, rows), 1) < row_count[0]
    return jnp.where(live, coulomb, 0.0).astype(BF16)


def solution(mesh):
    placed = (P(None, "pairs"), P("pairs", "aux"), P("aux", "pairs"), P("pairs"))
    return jax.shard_map(
        functools.partial(body, mesh.shape["pairs"]),
        mesh=mesh,
        in_specs=placed,
        out_specs=P("aux", "pairs"),
        check_vma=False,
    )
```

```python
import functools

import jax
import jax.numpy as jnp
from jax import lax
from jax.experimental import pallas as pl
from jax.experimental.pallas import tpu as pltpu
from jax.sharding import PartitionSpec as P

F32, BF16 = jnp.float32, jnp.bfloat16
MIB = 1 << 20


def digits_of(count):
    sizes = []
    while count > 1:
        size = 4 if count % 4 == 0 else 2
        sizes.append(size)
        count //= size
    return sizes


def largest_step(extent, limit, unit):
    return max(s for s in range(unit, limit + 1, unit) if extent % s == 0)


def swap(x, axis, count, mask):
    return lax.ppermute(x, axis, [(i, i ^ mask) for i in range(count)])


def params(used_bytes):
    return pltpu.CompilerParams(vmem_limit_bytes=used_bytes + 4 * MIB)


def in_hbm(x):
    return pltpu.with_memory_space_constraint(x, pltpu.HBM)


def in_vmem(x):
    return pltpu.with_memory_space_constraint(x, pltpu.VMEM)


def spec(space):
    return pl.BlockSpec(memory_space=space)


VMEM, HBM = pltpu.VMEM, pltpu.HBM


def field(info_ref, at):
    return info_ref[...][0, at]


def cost(flops, read):
    return pl.CostEstimate(flops=flops, bytes_accessed=read, transcendentals=0)


def slot_copies(digit, picks, per, tensor_ref, slots_ref, sems):
    step = slots_ref.shape[2]
    copies = []
    for at, pick in enumerate(picks):
        for j in range(per):
            slot = (digit ^ pick) * per + j
            copy = pltpu.make_async_copy(
                tensor_ref.at[:, pl.ds(pl.multiple_of(slot * step, 128), step)],
                slots_ref.at[slot],
                sems.at[at * per + j],
            )
            copy.start()
            copies.append((copy, slot))
    return copies


def fit_terms(masked, copies, per, slots_ref, outs):
    step = slots_ref.shape[2]
    for i, (copy, slot) in enumerate(copies):
        copy.wait()
        term = jnp.dot(masked, slots_ref[slot], preferred_element_type=F32)
        out, j = outs[i // per], i % per
        out[:, j * step : (j + 1) * step] = term.astype(out.dtype)


def fit_others_kernel(picks, per, info_ref, dens_hbm, tensor_ref, *rest):
    outs, (masked_ref, slots_ref, dens_ref, dens_sem, sems) = rest[: len(picks)], rest[len(picks) :]
    first = pltpu.make_async_copy(dens_hbm, dens_ref, dens_sem)
    first.start()
    copies = slot_copies(field(info_ref, 0) & len(picks), picks, per, tensor_ref, slots_ref, sems)
    first.wait()
    dens = dens_ref[...]
    live = lax.broadcasted_iota(jnp.int32, dens.shape, 1) < field(info_ref, 2)
    masked = jnp.where(live, dens.astype(F32), 0.0).astype(BF16)
    masked_ref[...] = masked
    fit_terms(masked, copies, per, slots_ref, outs)


def fit_others(picks, per, step, info, densities, tensor):
    rows, half_aux = tensor.shape
    k = densities.shape[0]
    n = len(picks) * per
    return pl.pallas_call(
        functools.partial(fit_others_kernel, picks, per),
        out_shape=[jax.ShapeDtypeStruct((k, per * step), BF16) for _ in picks]
        + [jax.ShapeDtypeStruct((k, rows), BF16), VMEM((half_aux // step, rows, step), BF16)],
        in_specs=[spec(VMEM), spec(HBM), spec(HBM)],
        out_specs=[spec(VMEM) for _ in range(len(picks) + 2)],
        scratch_shapes=[
            VMEM((k, rows), BF16),
            pltpu.SemaphoreType.DMA,
            pltpu.SemaphoreType.DMA((n,)),
        ],
        compiler_params=params(0),
        cost_estimate=cost(2 * k * rows * step * n, n * rows * step * 2),
    )(info, in_hbm(densities), in_hbm(tensor))


def row_copies(digit, picks, metric_ref, held, sems):
    depth = held[0].shape[0]
    copies = []
    for at, pick in enumerate(picks):
        first = pl.multiple_of((digit ^ pick) * depth, 128)
        copy = pltpu.make_async_copy(metric_ref.at[pl.ds(first, depth), :], held[at], sems.at[at])
        copy.start()
        copies.append(copy)
    return copies


def fit_own_kernel(
    per, top, info_ref, masked_ref, tensor_ref, metric_ref, before_ref, *rest
):
    out_ref, slots_ref, held_ref, sems, row_sems = rest
    digit = field(info_ref, 0) & top
    copies = slot_copies(digit, [0], per, tensor_ref, slots_ref, sems)
    (rows_in,) = row_copies(digit, [0], metric_ref, [held_ref], row_sems)
    fit_terms(masked_ref[...], copies, per, slots_ref, [out_ref])
    rows_in.wait()


def fit_own(per, top, step, info, masked, tensor, metric, slots):
    rows = tensor.shape[0]
    k = masked.shape[0]
    depth, width = per * step, metric.shape[1]
    return pl.pallas_call(
        functools.partial(fit_own_kernel, per, top),
        out_shape=[
            jax.ShapeDtypeStruct((k, per * step), F32),
            VMEM(slots.shape, BF16),
            VMEM((depth, width), BF16),
        ],
        in_specs=[spec(VMEM), spec(VMEM), spec(HBM), spec(HBM), spec(VMEM)],
        out_specs=[spec(VMEM) for _ in range(3)],
        scratch_shapes=[pltpu.SemaphoreType.DMA((per,)), pltpu.SemaphoreType.DMA((1,))],
        input_output_aliases={4: 1},
        compiler_params=params(0),
        cost_estimate=cost(2 * k * rows * step * per, (per * rows * step + depth * width) * 2),
    )(info, masked, in_hbm(tensor), in_hbm(metric), in_vmem(slots))


def fetch_kernel(picks, top, info_ref, metric_ref, own_ref, *rest):
    *held, same_ref, sems = rest
    copies = row_copies(field(info_ref, 0) & top, picks, metric_ref, held, sems)
    same_ref[...] = own_ref[...]
    for copy in copies:
        copy.wait()


def fetch(picks, top, depth, info, metric, own):
    width = metric.shape[1]
    return pl.pallas_call(
        functools.partial(fetch_kernel, picks, top),
        out_shape=[VMEM((depth, width), BF16) for _ in picks]
        + [jax.ShapeDtypeStruct(own.shape, own.dtype)],
        in_specs=[spec(VMEM), spec(HBM), spec(VMEM)],
        out_specs=[spec(VMEM) for _ in range(len(picks) + 1)],
        scratch_shapes=[pltpu.SemaphoreType.DMA((len(picks),))],
        compiler_params=params(0),
        cost_estimate=cost(0, len(picks) * depth * width * 2),
    )(info, in_hbm(metric), own)


def solve_own_kernel(
    picks, top, info_ref, metric_ref, fitted_ref, held_ref, out_ref, *rest
):
    *late, sems = rest
    copies = row_copies(field(info_ref, 0) & top, picks, metric_ref, late, sems)
    out_ref[...] = jnp.dot(fitted_ref[...], held_ref[...], preferred_element_type=F32)
    for copy in copies:
        copy.wait()


def solve_own(picks, top, info, metric, fitted, held):
    k, depth = fitted.shape
    width = metric.shape[1]
    return pl.pallas_call(
        functools.partial(solve_own_kernel, picks, top),
        out_shape=[jax.ShapeDtypeStruct((k, width), F32)]
        + [VMEM((depth, width), BF16) for _ in picks],
        in_specs=[spec(VMEM), spec(HBM), spec(VMEM), spec(VMEM)],
        out_specs=[spec(VMEM) for _ in range(len(picks) + 1)],
        scratch_shapes=[pltpu.SemaphoreType.DMA((len(picks),))],
        compiler_params=params(0),
        cost_estimate=cost(2 * k * depth * width, (1 + len(picks)) * depth * width * 2),
    )(info, in_hbm(metric), fitted, in_vmem(held))


def solve_others_kernel(count, low, info_ref, begun_ref, *rest):
    fitted, held, (out_ref, home_ref) = rest[:count], rest[count : 2 * count], rest[2 * count :]
    total = begun_ref[...]
    for x, rows in zip(fitted, held):
        total += jnp.dot(x[...], rows[...], preferred_element_type=F32)
    out_ref[...] = total
    home = field(info_ref, 0) >> (low.bit_length()) == field(info_ref, 1)
    home_ref[...] = jnp.where(home, total, 0.0)


def solve_others(low, info, begun, fitted, held):
    k, depth = fitted[0].shape
    width = held[0].shape[1]
    count = len(fitted)
    return pl.pallas_call(
        functools.partial(solve_others_kernel, count, low),
        out_shape=[VMEM((k, width), F32) for _ in range(2)],
        in_specs=[spec(VMEM)] + [spec(VMEM) for _ in range(1 + 2 * count)],
        out_specs=[spec(VMEM), spec(VMEM)],
        compiler_params=params(0),
        cost_estimate=cost(2 * k * depth * width * count, count * depth * width * 2),
    )(info, begun, *fitted, *[in_vmem(x) for x in held])


def split_for_cores(total, axis, core, outs):
    if len(outs) == 1:
        outs[0][...] = total
        return
    low, high = jnp.split(total, 2, axis)
    outs[0][...] = jnp.where(core == 0, low, high)
    outs[1][...] = jnp.where(core == 0, high, low)


def back_kernel(which, begun, low, info_ref, slots_ref, *rest):
    pieces, rest = rest[: len(which)], rest[len(which) :]
    if begun:
        start_ref, *outs = rest
        total = start_ref[...]
    else:
        outs = rest
        total = jnp.zeros((pieces[0].shape[1], slots_ref.shape[1]), F32)
    line, mine = field(info_ref, 0) & (low - 1), field(info_ref, 0) >> (low.bit_length() - 1)
    step = slots_ref.shape[2]
    for part, place in zip(pieces, which):
        per = part.shape[2] // step
        for i in range(part.shape[0]):
            for j in range(per):
                slot = i
                if place is not None:
                    slot = (((mine ^ i) & 1) * low + (line ^ place)) * per + j
                total += lax.dot_general(
                    part[i, :, j * step : (j + 1) * step],
                    slots_ref[slot],
                    (((1,), (1,)), ((), ())),
                    preferred_element_type=F32,
                )
    split_for_cores(total, 0, field(info_ref, 1), outs)


def back(which, low, info, slots, pieces, begun=None, split=True):
    rows = slots.shape[1]
    _, k, width = pieces[0].shape
    count = sum(part.shape[0] for part in pieces)
    extra = [] if begun is None else [begun]
    shapes = [(k // 2, rows)] * 2 if split else [(k, rows)]
    return pl.pallas_call(
        functools.partial(back_kernel, which, begun is not None, low),
        out_shape=[jax.ShapeDtypeStruct(shape, F32) for shape in shapes],
        in_specs=[spec(VMEM), spec(VMEM)] + [spec(VMEM) for _ in pieces + extra],
        out_specs=[spec(VMEM) for _ in shapes],
        compiler_params=params(0),
        cost_estimate=cost(2 * k * rows * width * count, count * rows * width * 2),
    )(info, in_vmem(slots), *pieces, *extra)


def body(n_pairs, densities, tensor, metric, row_count):
    rows, half_aux = tensor.shape
    block = metric.shape[1]
    sizes = digits_of(n_pairs)
    me = lax.axis_index("pairs")
    core = lax.axis_index("aux")
    first, rest = sizes[0], sizes[1:]
    info = jnp.stack([me.astype(jnp.int32), core.astype(jnp.int32), row_count[0]]).reshape(1, 3)
    width = half_aux // first

    others = list(range(first - 1, 0, -1))
    step = largest_step(width, 640, 128)
    per = width // step
    *sent, masked, slots = fit_others(others, per, step, info, densities, tensor)
    arrived = [swap(x, "pairs", n_pairs, pick) for x, pick in zip(sent, others)]
    total, slots, held = fit_own(per, first - 1, step, info, masked, tensor, metric, slots)
    for x in arrived:
        total = total + x.astype(F32)
    here = len(others) - 1
    stride = first
    for size in rest:
        sending = total.astype(BF16)
        arrived = [swap(sending, "pairs", n_pairs, pick * stride) for pick in range(1, size)]
        if stride == first:
            *rows_of, total = fetch(others[:here], first - 1, width, info, metric, total)
        for x in arrived:
            total = total + x.astype(F32)
        stride *= size
    fitted = total.astype(BF16)

    gathered = [swap(fitted, "pairs", n_pairs, pick) for pick in others]
    part, *late = solve_own(others[here:], first - 1, info, metric, fitted, held)
    last = sizes[-1]
    low = n_pairs // last
    part, at_home = solve_others(low, info, part, gathered, rows_of + late)

    homes = [(p, (p // low) // 2) for p in range(n_pairs)]
    across = 2 * low

    def send(x, pairs):
        return lax.ppermute(x, ("pairs", "aux"), [(p * 2 + c, q * 2 + d) for p, c, q, d in pairs])

    term = part.astype(BF16)
    first_pairs = [(p, 1 - c, p, c) for p, c in homes] + [(p, c, p ^ across, c) for p, c in homes]
    third_term = send(term, [(p, 1 - c, p ^ across, c) for p, c in homes])
    other_term = send(term, first_pairs)
    own = (at_home + third_term.astype(F32) + other_term.astype(F32)).astype(BF16)
    line_blocks = jnp.stack([own, swap(own, "pairs", n_pairs, low)])

    if block % step == 0 and len(sizes) == 2:
        arrived = [swap(line_blocks, "pairs", n_pairs, pick) for pick in others]
        (begun,) = back([0], low, info, slots, [line_blocks], split=False)
        for pick, x in zip(others[:-1], arrived[:-1]):
            (begun,) = back([pick], low, info, slots, [x], begun, split=False)
        keep, give = back(others[-1:], low, info, slots, arrived[-1:], begun)
    else:
        mine = me // low
        origin = [((mine ^ i) & 1) * low * block for i in range(2)]
        stride = 1
        lines = [me % low]
        pieces = line_blocks[None]
        for size in sizes[:-1]:
            arrived = [pieces] + [swap(pieces, "pairs", n_pairs, pick * stride) for pick in range(1, size)]
            lines = [x ^ (pick * stride) for pick in range(size) for x in lines]
            pieces = jnp.concatenate(arrived)
            stride *= size
        whole = jnp.zeros((densities.shape[0], half_aux), BF16)
        for at, x in enumerate(lines):
            for i in range(2):
                whole = lax.dynamic_update_slice_in_dim(
                    whole, pieces[at, i], origin[i] + x * block, 1
                )
        count = half_aux // step
        pieces = whole.reshape(-1, count, step).transpose(1, 0, 2)
        keep, give = back([None], low, info, slots, [pieces])

    coulomb = keep + swap(give, "aux", 2, 1)
    live = lax.broadcasted_iota(jnp.int32, (1, rows), 1) < row_count[0]
    return jnp.where(live, coulomb, 0.0).astype(BF16)


def solution(mesh):
    placed = (P(None, "pairs"), P("pairs", "aux"), P("aux", "pairs"), P("pairs"))
    return jax.shard_map(
        functools.partial(body, mesh.shape["pairs"]),
        mesh=mesh,
        in_specs=placed,
        out_specs=P("aux", "pairs"),
        check_vma=False,
    )
```
